32 devices in a mesh: dp: 16 (over z, y, x), tensor: 2 (over core).
Axes of the slice: x: 2, y: 2, z: 4, core: 2. Of those that a mesh axis runs over, the one named last changes fastest.
Arguments:
- layer_input: float32 [6144, 1536], P(('dp', 'tensor')), may hold values from -6 to 6
- output_grad: float32 [6144, 1536], P(('dp', 'tensor')), may hold values from -6 to 6
- seq_lengths: int32 [16, 4], P('dp'), may hold values from 0 to 384, as said below
- gains_biases: float32 [5120], P(('dp', 'tensor')), may hold values from -0.9 to 1.4, as said below
- gains_moment: float32 [5120], P(('dp', 'tensor'))
- gains_second: float32 [5120], P(('dp', 'tensor')), as said below
- qkv_weight: float32 [1536, 2, 1024], P('dp', 'tensor'), may hold values from -0.21875 to 0.21875
- qkv_moment: float32 [1536, 2, 1024], P('dp', 'tensor'), may hold values from -96 to 96
- qkv_second: float32 [1536, 2, 1024], P('dp', 'tensor'), may hold values from 18.432 to 73.728
- out_weight: float32 [1536, 1536], P('dp', 'tensor'), may hold values from -0.625 to 0.625
- out_moment: float32 [1536, 1536], P('dp', 'tensor'), may hold values from -20 to 20
- out_second: float32 [1536, 1536], P('dp', 'tensor'), may hold values from 0.79872 to 3.19488
- gate_up_weight: float32 [1536, 2, 8960], P('dp', None, 'tensor'), may hold values from -0.15625 to 0.15625
- gate_up_moment: float32 [1536, 2, 8960], P('dp', None, 'tensor'), may hold values from -14 to 14
- gate_up_second: float32 [1536, 2, 8960], P('dp', None, 'tensor'), may hold values from 0.43008 to 1.72032
- down_weight: float32 [1536, 8960], P('dp', 'tensor'), may hold values from -0.0625 to 0.0625
- down_moment: float32 [1536, 8960], P('dp', 'tensor'), may hold values from -28 to 28
- down_second: float32 [1536, 8960], P('dp', 'tensor'), may hold values from 1.8432 to 7.3728
Outputs:
- layer_output: float32 [6144, 1536], P(('dp', 'tensor'))
- input_grad: float32 [6144, 1536], P(('dp', 'tensor'))
- gains_moment_new: float32 [5120], P(('dp', 'tensor'))
- gains_second_new: float32 [5120], P(('dp', 'tensor'))
- gains_biases_new: float32 [5120], P(('dp', 'tensor'))
- qkv_moment_new: float32 [1536, 2, 1024], P('dp', 'tensor')
- qkv_second_new: float32 [1536, 2, 1024], P('dp', 'tensor')
- qkv_weight_new: float32 [1536, 2, 1024], P('dp', 'tensor')
- out_moment_new: float32 [1536, 1536], P('dp', 'tensor')
- out_second_new: float32 [1536, 1536], P('dp', 'tensor')
- out_weight_new: float32 [1536, 1536], P('dp', 'tensor')
- gate_up_moment_new: float32 [1536, 2, 8960], P('dp', None, 'tensor')
- gate_up_second_new: float32 [1536, 2, 8960], P('dp', None, 'tensor')
- gate_up_weight_new: float32 [1536, 2, 8960], P('dp', None, 'tensor')
- down_moment_new: float32 [1536, 8960], P('dp', 'tensor')
- down_second_new: float32 [1536, 8960], P('dp', 'tensor')
- down_weight_new: float32 [1536, 8960], P('dp', 'tensor')
The draws below stay inside these ranges and needn't reach their ends.
Inputs may be any that keep to these rules, and one draw needn't show every extreme that they name: `seq_lengths`: each row sums to at most 384; in one row the first slot is empty and the second holds a single sequence of exactly 384; every row sums to 240 or more; in every row one sequence holds both buffer rows 191 and 192; a length 0 marks an empty slot. `gains_biases`: the gains lie within 0.6 to 1.4, the bias entries within -0.9 to 0.9. `gains_second`: Positive.
All inputs are finite; a program needn't handle non-finite values.
Results may differ from the reference program's by a relative error of at most 0.014.
The reference program's roundings to bfloat16 on the way count: a program that leaves them out, or rounds other values in their place, can miss the bound.
Values may be sent and summed in bfloat16 or wider, within the bound.
A program may use at most 320 MiB of HBM per device.

```python
import math
import jax
import jax.numpy as jnp
from jax import lax

D = 1536
H = 12
KVH = 2
HD = 128
FF = 8960
QPK = 6
GROUP = 1024
SMALL = 5120
TOK_DEV = 384
STEP = 10
TOKENS = 6144
N_DP = 16


def small_scales():
    return jnp.concatenate([jnp.full((D,), 8.0, jnp.float32), jnp.full((D,), 0.7, jnp.float32), jnp.full((SMALL - 2 * D,), 3.0, jnp.float32)]) * TOKENS


def draw_seq_lengths(key, part):
    key = jax.random.fold_in(key, 11)
    keys = jax.random.split(key, 5)
    half_rows = TOK_DEV // 2
    totals = jax.random.randint(keys[0], (N_DP,), 5 * TOK_DEV // 8, TOK_DEV + 1)
    fullest = jax.random.randint(keys[1], (), 0, N_DP)
    is_full = jnp.arange(N_DP) == fullest
    totals = jnp.where(is_full, TOK_DEV, totals).astype(jnp.int32)
    first_end = jax.random.randint(keys[2], (N_DP,), 0, half_rows)
    second_end = jax.random.randint(keys[3], (N_DP,), half_rows + 1, totals + 1)
    third_end = jax.random.randint(keys[4], (N_DP,), second_end, totals + 1)
    first_end = jnp.where(is_full, 0, first_end)
    second_end = jnp.where(is_full, TOK_DEV, second_end)
    third_end = jnp.where(is_full, TOK_DEV, third_end)
    seq_ends = jnp.stack([first_end, second_end, third_end, totals], 1).astype(jnp.int32)
    seq_starts = jnp.concatenate([jnp.zeros((N_DP, 1), jnp.int32), seq_ends[:, :-1]], 1)
    return (seq_ends - seq_starts).astype(jnp.int32)


def draw_gains_biases(key, part):
    key = jax.random.fold_in(key, 12)
    keys = jax.random.split(key, 2)
    gains = jax.random.uniform(keys[0], (2 * D,), jnp.float32, 0.6, 1.4)
    biases = 0.3 * jax.random.truncated_normal(keys[1], -3.0, 3.0, (SMALL - 2 * D,), jnp.float32)
    return jnp.concatenate([gains, biases])


def draw_gains_moment(key, part):
    key = jax.random.fold_in(key, 13)
    noise = jax.random.truncated_normal(key, -4.0, 4.0, (SMALL,), jnp.float32)
    return 0.11 * jnp.sqrt(small_scales()) * noise


def draw_gains_second(key, part):
    key = jax.random.fold_in(key, 14)
    spread = jax.random.uniform(key, (SMALL,), jnp.float32, 0.0, math.log(4.0))
    return 0.001 * small_scales() * jnp.exp(spread)


def block_levels(key, dims, cuts, least, high):
    factor_of = 1.0
    for axis_at, shards_of in cuts:
        draws = jax.random.uniform(jax.random.fold_in(jax.random.fold_in(key, 6), axis_at), (shards_of,), jnp.float32, least / len(cuts), high / len(cuts))
        factor_of = factor_of * jnp.repeat(jnp.exp(draws), dims[axis_at] // shards_of).reshape((-1,) + (1,) * (len(dims) - 1 - axis_at))
    return factor_of


def centred(rng, shape, scale, limit, shards=(), kind=jnp.bfloat16):
    array = scale * jax.random.normal(rng, shape, jnp.float32)
    if shards:
        array = array * block_levels(rng, shape, shards, -0.22, 0.18)
    return jnp.clip(array, -limit, limit).astype(kind)


def setup_inputs(seed: int = 0) -> dict:
    arg_keys = jax.random.split(jax.random.key(seed), 19)
    return {
        "layer_input": centred(arg_keys[0], (TOKENS, D), 1.0, 6.0, ((0, 32),), jnp.float32),
        "output_grad": centred(arg_keys[1], (TOKENS, D), 1.0, 6.0, ((0, 32),), jnp.float32),
        "seq_lengths": draw_seq_lengths(jax.random.fold_in(arg_keys[18], 71), 0),
        "gains_biases": draw_gains_biases(jax.random.fold_in(arg_keys[18], 71), 0),
        "gains_moment": draw_gains_moment(jax.random.fold_in(arg_keys[18], 71), 0),
        "gains_second": draw_gains_second(jax.random.fold_in(arg_keys[18], 71), 0),
        "qkv_weight": centred(arg_keys[6], (D, KVH, GROUP), (D // 2) ** -0.5, 0.21875, ((0, 16), (1, 2)), jnp.float32),
        "qkv_moment": centred(arg_keys[7], (D, KVH, GROUP), (0.19 * TOKENS ** 0.5), 96.0, ((0, 16), (1, 2)), jnp.float32),
        "qkv_second": jnp.clip(jnp.exp(math.log(73.728) - 1.3862944 * jax.random.uniform(arg_keys[8], (D, KVH, GROUP), jnp.float32) ** block_levels(arg_keys[8], (D, KVH, GROUP), ((0, 16), (1, 2)), -0.2, 0.2)), 18.432, 73.728),
        "out_weight": centred(arg_keys[9], (D, H * HD), (H * HD // 16) ** -0.5, 0.625, ((0, 16), (1, 2)), jnp.float32),
        "out_moment": centred(arg_keys[10], (D, H * HD), (0.04 * TOKENS ** 0.5), 20.0, ((0, 16), (1, 2)), jnp.float32),
        "out_second": jnp.clip(jnp.exp(math.log(3.19488) - 1.3862944 * jax.random.uniform(arg_keys[11], (D, H * HD), jnp.float32) ** block_levels(arg_keys[11], (D, H * HD), ((0, 16), (1, 2)), -0.2, 0.2)), 0.79872, 3.19488),
        "gate_up_weight": centred(arg_keys[12], (D, 2, FF), D ** -0.5, 0.15625, ((0, 16), (2, 2)), jnp.float32),
        "gate_up_moment": centred(arg_keys[13], (D, 2, FF), (0.03 * TOKENS ** 0.5), 14.0, ((0, 16), (2, 2)), jnp.float32),
        "gate_up_second": jnp.clip(jnp.exp(math.log(1.72032) - 1.3862944 * jax.random.uniform(arg_keys[14], (D, 2, FF), jnp.float32) ** block_levels(arg_keys[14], (D, 2, FF), ((0, 16), (2, 2)), -0.2, 0.2)), 0.43008, 1.72032),
        "down_weight": centred(arg_keys[15], (D, FF), FF ** -0.5, 0.0625, ((0, 16), (1, 2)), jnp.float32),
        "down_moment": centred(arg_keys[16], (D, FF), (0.06 * TOKENS ** 0.5), 28.0, ((0, 16), (1, 2)), jnp.float32),
        "down_second": jnp.clip(jnp.exp(math.log(7.3728) - 1.3862944 * jax.random.uniform(arg_keys[17], (D, FF), jnp.float32) ** block_levels(arg_keys[17], (D, FF), ((0, 16), (1, 2)), -0.2, 0.2)), 1.8432, 7.3728),
    }


NORM_EPS = 1e-06
ROPE_THETA = 1000000.0
MASK_VALUE = -1e+30
FIRST_DECAY = 0.9
SECOND_DECAY = 0.999
ADAM_EPS = 1e-08
WEIGHT_DECAY = 0.1
RATE_SMALL = 0.3
RATE_PROJECT = 0.04
RATE_OUTPUT = 0.1
RATE_FEED = 0.03
RATE_DOWN = 0.015
PRECISE = lax.Precision.HIGHEST

@jax.custom_vjp
def low(v):
    return lax.optimization_barrier(v.astype(jnp.bfloat16)).astype(jnp.float32)

@jax.custom_vjp
def low_back(v):
    return v

def low_keep(v):
    return (low(v), None)

def low_pass(kept, grad):
    return (grad,)

def back_keep(v):
    return (v, None)

def back_low(kept, grad):
    return (low(grad),)
low.defvjp(low_keep, low_pass)
low_back.defvjp(back_keep, back_low)

def layout(lengths):
    row_index = jnp.arange(TOK_DEV, dtype=jnp.int32)
    seq_ends = jnp.cumsum(lengths).astype(jnp.int32)
    passed = (row_index[:, None] >= seq_ends[None, :]).astype(jnp.int32)
    segment = lax.optimization_barrier(jnp.sum(passed, axis=1)).astype(jnp.int32)
    seq_start = lax.optimization_barrier(jnp.sum(passed * lengths[None, :], axis=1)).astype(jnp.int32)
    live_rows = (row_index < seq_ends[-1]).astype(jnp.float32)
    return (segment, row_index - seq_start, live_rows)

def rotary(position, head_dim):
    frequency = ROPE_THETA ** (-jnp.arange(0, head_dim, 2, dtype=jnp.float32) / head_dim)
    angles = position.astype(jnp.float32)[:, None] * frequency[None, :]
    cosine_table = jnp.concatenate([jnp.cos(angles), jnp.cos(angles)], 1)
    sine_table = jnp.concatenate([jnp.sin(angles), jnp.sin(angles)], 1)
    return (cosine_table, sine_table)

def rotate(vector, cosine_table, sine_table):
    half_width = vector.shape[-1] // 2
    turned = jnp.concatenate([-vector[..., half_width:], vector[..., :half_width]], -1)
    return vector * cosine_table + turned * sine_table

def rms_norm(vector, gain_vec):
    return vector * lax.rsqrt(lax.optimization_barrier(jnp.mean(vector * vector, axis=-1, keepdims=True)) + NORM_EPS) * gain_vec

def buffer_forward(layer_in, lengths, small_vals, qkv_low, out_low, gate_up_low, down_low):
    segment, position, live_rows = layout(lengths)
    cosine_table, sine_table = rotary(position, HD)
    gain_attn = small_vals[:D]
    gain_mlp = small_vals[D:2 * D]
    bias_table = small_vals[2 * D:].reshape(KVH, GROUP)
    normed = low(rms_norm(layer_in, gain_attn))
    projected = low_back(jnp.einsum('td,dgc->tgc', normed, qkv_low, precision=PRECISE) + bias_table)
    queries = projected[:, :, :QPK * HD].reshape(TOK_DEV, KVH, QPK, HD)
    queries = low(rotate(queries, cosine_table[:, None, None, :], sine_table[:, None, None, :]))
    key_heads = low(rotate(projected[:, :, QPK * HD:(QPK + 1) * HD], cosine_table[:, None, :], sine_table[:, None, :]))
    values = low(projected[:, :, (QPK + 1) * HD:])
    row_order = jnp.arange(TOK_DEV, dtype=jnp.int32)
    allowed = (segment[:, None] == segment[None, :]) & (row_order[None, :] <= row_order[:, None])
    scores = low_back(jnp.einsum('tgjc,sgc->gjts', queries, key_heads, precision=PRECISE) * HD ** (-0.5))
    scores = jnp.where(allowed, scores, MASK_VALUE)
    top_score = lax.optimization_barrier(jnp.max(scores, axis=-1, keepdims=True))
    exp_scores = jnp.exp(scores - top_score)
    attn_probs = low(exp_scores / lax.optimization_barrier(jnp.sum(exp_scores, axis=-1, keepdims=True)))
    attended = jnp.einsum('gjts,sgc->tgjc', attn_probs, values, precision=PRECISE).reshape(TOK_DEV, H * HD)
    attended = low_back(low(attended))
    branch = low_back(jnp.dot(attended, out_low.T, precision=PRECISE))
    middle = layer_in + branch
    normed_mid = low(rms_norm(middle, gain_mlp))
    gate_up = low_back(jnp.einsum('td,dkf->tkf', normed_mid, gate_up_low, precision=PRECISE))
    hidden = low(jax.nn.silu(gate_up[:, 0]) * gate_up[:, 1])
    feed = low_back(jnp.dot(hidden, down_low.T, precision=PRECISE))
    return (middle + feed) * live_rows[:, None]

def adam_update(weight, moment, second, gradient, rate, decay):
    moment_new = FIRST_DECAY * moment + (1.0 - FIRST_DECAY) * gradient
    second_new = SECOND_DECAY * second + (1.0 - SECOND_DECAY) * gradient * gradient
    moment_hat = moment_new / (1.0 - FIRST_DECAY ** STEP)
    second_hat = second_new / (1.0 - SECOND_DECAY ** STEP)
    weight_new = weight - rate * (moment_hat / (jnp.sqrt(second_hat) + ADAM_EPS) + decay * weight)
    return (moment_new, second_new, weight_new)

def reference(layer_input, output_grad, seq_lengths, gains_biases, gains_moment, gains_second, qkv_weight, qkv_moment, qkv_second, out_weight, out_moment, out_second, gate_up_weight, gate_up_moment, gate_up_second, down_weight, down_moment, down_second):
    checked = jax.checkpoint(buffer_forward)

    def forward(layer_in, small_vals, qkv_full, out_full, gate_up_full, down_full):
        qkv_low = low(qkv_full)
        out_low = low(out_full)
        gate_up_low = low(gate_up_full)
        down_low = low(down_full)

        def scan_step(scan_carry, pieces):
            return (scan_carry, checked(pieces[0], pieces[1], small_vals, qkv_low, out_low, gate_up_low, down_low))
        _, outputs = lax.scan(scan_step, jnp.zeros((), jnp.float32), (layer_in.reshape(N_DP, TOK_DEV, D), seq_lengths))
        return outputs.reshape(N_DP * TOK_DEV, D)
    layer_output, pullback = jax.vjp(forward, layer_input, gains_biases, qkv_weight, out_weight, gate_up_weight, down_weight)
    input_grad, grad_small, grad_qkv, grad_out, grad_gate_up, grad_down = pullback(output_grad)
    small_m, small_s, small_w = adam_update(gains_biases, gains_moment, gains_second, grad_small, RATE_SMALL, 0.0)
    qkv_m, qkv_s, qkv_w = adam_update(qkv_weight, qkv_moment, qkv_second, grad_qkv, RATE_PROJECT, WEIGHT_DECAY)
    out_m, out_s, out_w = adam_update(out_weight, out_moment, out_second, grad_out, RATE_OUTPUT, WEIGHT_DECAY)
    feed_m, feed_s, feed_w = adam_update(gate_up_weight, gate_up_moment, gate_up_second, grad_gate_up, RATE_FEED, WEIGHT_DECAY)
    down_m, down_s, down_w = adam_update(down_weight, down_moment, down_second, grad_down, RATE_DOWN, WEIGHT_DECAY)
    return (layer_output, input_grad, small_m, small_s, small_w, qkv_m, qkv_s, qkv_w, out_m, out_s, out_w, feed_m, feed_s, feed_w, down_m, down_s, down_w)
```

```python
import functools

import jax
import jax.numpy as jnp
from jax import lax
from jax.experimental import pallas as pl
from jax.experimental.pallas import tpu as pltpu
from jax.experimental.layout import Layout, with_layout_constraint
from jax.sharding import PartitionSpec as P

HD = 128
STEP = 10
LANES = 128

NORM_EPS = 1e-06
ROPE_THETA = 1000000.0
MASK_VALUE = -1e30
FIRST_DECAY = 0.9
SECOND_DECAY = 0.999
ADAM_EPS = 1e-08
WEIGHT_DECAY = 0.1
RATE_SMALL = 0.3
RATE_PROJECT = 0.04
RATE_OUTPUT = 0.1
RATE_FEED = 0.03
RATE_DOWN = 0.015

BF16 = jnp.bfloat16
F32 = jnp.float32


def layout(lengths, buffer_rows):
    row_index = jnp.arange(buffer_rows, dtype=jnp.int32)
    seq_ends = jnp.cumsum(lengths)
    passed = (row_index[:, None] >= seq_ends[None, :]).astype(jnp.int32)
    segment = jnp.sum(passed, axis=1)
    seq_start = jnp.sum(passed * lengths[None, :], axis=1)
    live_rows = (row_index < seq_ends[-1]).astype(jnp.float32)
    return (segment, row_index - seq_start, live_rows)


def rotary(position, head_dim):
    frequency = ROPE_THETA ** (-jnp.arange(0, head_dim, 2, dtype=jnp.float32) / head_dim)
    angles = position.astype(jnp.float32)[:, None] * frequency[None, :]
    cosine_table = jnp.concatenate([jnp.cos(angles), jnp.cos(angles)], 1)
    sine_table = jnp.concatenate([jnp.sin(angles), jnp.sin(angles)], 1)
    return (cosine_table, sine_table)


def rotate(vector, cosine_table, sine_table):
    half_width = vector.shape[-1] // 2
    turned = jnp.concatenate([-vector[..., half_width:], vector[..., :half_width]], -1)
    return vector * cosine_table + turned * sine_table


def unrotate(gradient, cosine_table, sine_table):
    half_width = gradient.shape[-1] // 2
    turned = gradient * sine_table
    return gradient * cosine_table + jnp.concatenate(
        [turned[..., half_width:], -turned[..., :half_width]], -1
    )


def norm_back(grad_normed, unit_rows, inv_rows, gain_vec):
    scaled = grad_normed * gain_vec
    return inv_rows * (scaled - unit_rows * jnp.mean(scaled * unit_rows, axis=1, keepdims=True))


def adam_update(weight, moment, second, gradient, rate, decay):
    moment_new = FIRST_DECAY * moment + (1.0 - FIRST_DECAY) * gradient
    second_new = SECOND_DECAY * second + (1.0 - SECOND_DECAY) * gradient * gradient
    moment_hat = moment_new / (1.0 - FIRST_DECAY**STEP)
    second_hat = second_new / (1.0 - SECOND_DECAY**STEP)
    weight_new = weight - rate * (moment_hat / (jnp.sqrt(second_hat) + ADAM_EPS) + decay * weight)
    return (moment_new, second_new, weight_new)


def dot(a, b, dims):
    return lax.dot_general(a, b, (dims, ((), ())), preferred_element_type=F32)


PLANES = 4
RING = 4
MESH = pl.DeviceIdType.MESH
MIB = 1024 * 1024


class Here:
    def __init__(self, members):
        self.n = RING
        me = lax.axis_index("dp")
        self.core = lax.axis_index("tensor")
        self.members = members
        self.member = lax.rem(me, members)
        group = lax.div(me, members)
        self.plane = lax.div(group, RING)
        self.index = lax.rem(group, RING)
        odd, half = lax.rem(self.index, 2), lax.div(self.index, 2)
        self.spot = (1 - odd) * half + odd * (RING - 1 - half)
        self.right = self.dp(self.plane, self.at(1))
        self.left = self.dp(self.plane, self.at(RING - 1))
        self.above = self.dp(self.plane + 1, self.index)
        self.below = self.dp(self.plane - 1, self.index)
        self.other = 1 - self.core

    def dp(self, plane, index):
        return (plane * RING + index) * self.members + self.member

    def at(self, s):
        spot = lax.rem(self.spot + s, self.n)
        far = lax.div(spot, self.n // 2)
        return (1 - far) * 2 * spot + far * (2 * (self.n - 1 - spot) + 1)

    def back(self, s):
        return self.at((self.n - s) % self.n)

    def plane_back(self, r):
        return lax.rem(self.plane + PLANES - r, PLANES)

    def dp_ahead(self, k):
        return self.dp(lax.rem(self.plane + k, PLANES), self.index)

    def hops(self, r):
        half = self.n // 2
        return (half, half - 1) if r % 2 == 0 else (half - 1, half)

    def barrier(self, ring=True):
        sem = pltpu.get_barrier_semaphore()
        partners = [{"dp": self.dp_ahead(k)} for k in range(1, PLANES)] + [{"tensor": self.other}]
        if ring:
            partners += [{"dp": self.right}, {"dp": self.left}]
        for partner in partners:
            pl.semaphore_signal(sem, inc=1, device_id=partner, device_id_type=MESH)
        pl.semaphore_wait(sem, len(partners))


def remote(src, dst, send, recv, **to):
    return pltpu.make_async_remote_copy(
        src_ref=src, dst_ref=dst, send_sem=send, recv_sem=recv, device_id=to, device_id_type=MESH
    )


class LineGather:
    def __init__(self, here, own, slot, send, recv):
        self.here, self.own, self.slot, self.send, self.recv = here, own, slot, send, recv

    def copy(self, way, d):
        here = self.here
        origin = here.plane - d if way == 0 else here.plane + d
        src = self.own if d == 0 else self.slot(origin)
        to = here.above if way == 0 else here.below
        return remote(src, self.slot(origin), self.send.at[way, d], self.recv.at[way, d + 1], dp=to)

    def has_next(self, way):
        return self.here.plane + 1 < PLANES if way == 0 else self.here.plane > 0

    def comes(self, way, d):
        return self.here.plane >= d if way == 0 else self.here.plane + d < PLANES

    def start(self):
        for way in range(2):
            pl.when(self.has_next(way))(self.copy(way, 0).start)

    def arrive(self, way, d, then=None):
        @pl.when(self.comes(way, d))
        def _():
            here = self.here
            origin = here.plane - d if way == 0 else here.plane + d
            from_dp = here.below if way == 0 else here.above
            landed = self.slot(origin)
            remote(landed, landed, self.send.at[way, d], self.recv.at[way, d], dp=from_dp).wait_recv()
            if d + 1 < PLANES:
                pl.when(self.has_next(way))(self.copy(way, d).start)
            if then is not None:
                then(d if way == 0 else PLANES - d)

    def finish(self):
        for way in range(2):
            for d in range(PLANES - 1):
                pl.when(self.comes(way, d) & self.has_next(way))(self.copy(way, d).wait_send)


class RingGather:
    def __init__(self, here, r, own, slot, send, recv):
        self.here, self.own, self.slot, self.send, self.recv = here, own, slot, send, recv
        self.hops = here.hops(r)

    def copy(self, way, d):
        here = self.here
        origin = here.back(d) if way == 0 else here.at(d)
        src = self.own if d == 0 else self.slot(origin)
        to = here.right if way == 0 else here.left
        return remote(src, self.slot(origin), self.send.at[way, d], self.recv.at[way, d + 1], dp=to)

    def start(self):
        for way in range(2):
            if self.hops[way]:
                self.copy(way, 0).start()

    def arrive(self, d):
        here = self.here
        for way in range(2):
            if d <= self.hops[way]:
                landed = self.slot(here.back(d) if way == 0 else here.at(d))
                remote(
                    landed, landed, self.send.at[way, d - 1], self.recv.at[way, d], dp=here.right
                ).wait_recv()
                if d < self.hops[way]:
                    self.copy(way, d).start()

    def finish(self):
        for way in range(2):
            for d in range(self.hops[way]):
                self.copy(way, d).wait_send()


class LineSum:
    def __init__(self, here, addend, landing, send, recv):
        self.here, self.addend, self.landing, self.send, self.recv = here, addend, landing, send, recv

    def copy(self, way, d, slot):
        to = self.here.below if way == 0 else self.here.above
        return remote(slot, self.landing(way, d), self.send.at[way, d], self.recv.at[way, d], dp=to)

    def goes(self, way, d):
        return self.here.plane >= d if way == 0 else self.here.plane + d < PLANES

    def has_prior(self, way):
        return self.here.plane + 1 < PLANES if way == 0 else self.here.plane > 0

    def wait(self, way, d):
        slot = self.landing(way, d)
        to = self.here.below if way == 0 else self.here.above
        remote(slot, slot, self.send.at[way, d], self.recv.at[way, d], dp=to).wait_recv()

    def step(self, way, d):
        here = self.here
        target = here.plane - d if way == 0 else here.plane + d

        @pl.when(self.goes(way, d))
        def _():
            if d + 1 < PLANES:

                @pl.when(self.has_prior(way))
                def _():
                    slot = self.landing(way, d + 1)
                    self.wait(way, d + 1)
                    slot[...] = (slot[...].astype(F32) + self.addend(target)).astype(BF16)
                    self.copy(way, d, slot).start()

            @pl.when(jnp.logical_not(self.has_prior(way)))
            def _():
                slot = self.landing(way, d)
                slot[...] = self.addend(target).astype(BF16)
                self.copy(way, d, slot).start()

    def result(self, out):
        out[...] = self.addend(self.here.plane)
        for way in range(2):

            @pl.when(self.has_prior(way))
            def _():
                self.wait(way, 1)
                out[...] = out[...] + self.landing(way, 1)[...].astype(F32)

    def finish(self):
        for way in range(2):
            for d in range(1, PLANES):
                pl.when(self.goes(way, d))(self.copy(way, d, self.landing(way, d)).wait_send)


class RingSum:
    def __init__(self, here, r, partial, nearby, own, land, send, recv):
        self.here, self.partial, self.nearby, self.own = here, partial, nearby, own
        self.land, self.send, self.recv = land, send, recv
        self.ahead = r % 2 == 0

    def next_long(self):
        return self.here.at(1) if self.ahead else self.here.back(1)

    def copy(self, k):
        here = self.here
        if k == 0:
            src = self.partial(here.at(2))
        elif k == 1:
            src = self.land.at[0]
        else:
            src = self.partial(here.back(1) if self.ahead else here.at(1))
        to = here.right if self.ahead == (k < 2) else here.left
        return remote(src, self.land.at[k], self.send.at[k], self.recv.at[k], dp=to)

    def start(self):
        self.copy(0).start()
        self.copy(2).start()

    def step(self):
        self.copy(0).wait_recv()
        slot = self.land.at[0]
        slot[...] = (slot[...].astype(F32) + self.nearby[...].astype(F32)).astype(slot.dtype)
        self.copy(1).start()

    def result(self):
        self.copy(1).wait_recv()
        self.copy(2).wait_recv()
        return (
            self.own[...].astype(F32) + self.land[1].astype(F32) + self.land[2].astype(F32)
        )

    def finish(self):
        for k in range(3):
            self.copy(k).wait_send()


class FarRingSum(RingSum):
    def __init__(self, here, r, partial, passing, land, send, recv, load):
        super().__init__(here, r, partial, None, None, land, send, recv)
        self.passing, self.load = passing, load

    def copy(self, k):
        if k != 1:
            return super().copy(k)
        here = self.here
        to = here.right if self.ahead else here.left
        return remote(self.passing, self.land.at[1], self.send.at[1], self.recv.at[1], dp=to)

    def bring(self, k, to):
        return pltpu.make_async_copy(self.land.at[k], to, self.load.at[k])

    def step(self):
        self.copy(0).wait_recv()
        self.bring(0, self.passing).start()
        self.bring(0, self.passing).wait()
        here, nearby = self.passing, self.nearby
        here[...] = (here[...].astype(F32) + nearby[...].astype(F32)).astype(here.dtype)
        self.copy(1).start()

    def result(self, first, second):
        self.copy(1).wait_recv()
        self.bring(1, first).start()
        self.copy(2).wait_recv()
        self.bring(2, second).start()
        self.bring(1, first).wait()
        self.bring(2, second).wait()
        return self.own[...].astype(F32) + first[...].astype(F32) + second[...].astype(F32)

    def finish(self, passed=True):
        for k in (0, 1, 2) if passed else (0, 2):
            self.copy(k).wait_send()


def line_order():
    return [(way, d) for d in range(1, PLANES) for way in range(2)]


def turn(v, cosine, signed_sine):
    return v * cosine + pltpu.roll(v, HD // 2, 1) * signed_sine


def turn_back(v, cosine, signed_sine):
    return v * cosine - pltpu.roll(v, HD // 2, 1) * signed_sine


def fold(v):
    return jnp.sum(v.reshape(v.shape[0] // 8, 8, v.shape[1]), axis=0)


def layer_kernel(
    members,
    small_ref,
    attn_ref,
    feed_ref,
    back_low_ref,
    back_ref,
    x_ref,
    cos_ref,
    sin_ref,
    mask_ref,
    live_ref,
    layer_out,
    input_grad,
    small_sum,
    qkv_sum,
    out_sum,
    feed_new,
    attn_hbm,
    grads_hbm,
    grads_land,
    qkv_land,
    out_land,
    small_row,
    normed,
    qkv,
    attended,
    mid_sum,
    small_land,
    weights,
    tokens,
    backs,
    branch_send,
    part,
    part_land,
    part_line,
    branch_all,
    qkv_line_land,
    out_line_land,
    gain_row,
    small_part,
    small_pair_land,
    small_ring_land,
    small_plane,
    small_line_land,
    ready_sem,
    line_send,
    line_recv,
    gather_send,
    gather_recv,
    feed_ring_send,
    feed_ring_recv,
    cross_send,
    cross_recv,
    pair_send,
    pair_recv,
    sum_send,
    sum_recv,
    sum_load,
    small_send,
    small_recv,
    keep_sem,
    load_sem,
    stage_sem,
):
    here = Here(members)
    p, i, c, other = here.plane, here.index, here.core, here.other
    rows, width = x_ref.shape
    cols = qkv.shape[1]
    heads = cols // HD - 2
    small_n = small_row.shape[1] // (2 * PLANES * RING)
    keeps = [
        pltpu.make_async_copy(small_ref, small_land.at[c, p, i], keep_sem.at[0]),
        pltpu.make_async_copy(attn_ref, attn_hbm.at[p, i], keep_sem.at[1]),
        pltpu.make_async_copy(feed_ref.at[p], weights.at[:, p, i], keep_sem.at[2]),
        pltpu.make_async_copy(back_low_ref, backs.at[p, c], keep_sem.at[3]),
    ]
    for keep in keeps:
        keep.start()
    here.barrier()

    def ring(k, r, own, slot):
        return RingGather(here, r, own, slot, gather_send.at[k, r], gather_recv.at[k, r])

    small_line = LineGather(
        here, small_ref, lambda q: small_land.at[c, q, i], line_send.at[0], line_recv.at[0]
    )
    attn_line = LineGather(
        here, attn_ref, lambda q: attn_hbm.at[q, i], line_send.at[1], line_recv.at[1]
    )
    back_line = LineGather(
        here, back_low_ref, lambda q: backs.at[q, c], line_send.at[2], line_recv.at[2]
    )
    token_line = LineGather(
        here, tokens.at[p, c], lambda q: tokens.at[q, c], line_send.at[3], line_recv.at[3]
    )
    near = [p, 1 + lax.rem(p, 2), lax.rem(2 + 3 * p, 5), 3 * (1 - lax.div(p, 2))]
    tiles = [(0, 512), (512, 1024), (1024, weights.shape[-1])]
    small_rings, attn_rings, feed_rings = [], [], []
    for r in range(PLANES):
        q = here.plane_back(r)
        small_rings.append(
            ring(0, r, small_ref if r == 0 else small_land.at[c, q, i], lambda j, q=q: small_land.at[c, q, j])
        )
        attn_rings.append(
            ring(1, r, attn_ref if r == 0 else attn_hbm.at[q, i], lambda j, q=q: attn_hbm.at[q, j])
        )
        feed_rings.append([])
        for t, (lo, hi) in enumerate(tiles):
            own = feed_ref.at[p, :, :, lo:hi] if r == 0 else weights.at[:, q, i, :, lo:hi]
            feed_rings[r].append(
                RingGather(
                    here,
                    r,
                    own,
                    lambda j, q=q, lo=lo, hi=hi: weights.at[:, q, j, :, lo:hi],
                    feed_ring_send.at[t, r],
                    feed_ring_recv.at[t, r],
                )
            )

    def cross(k, t):
        q = lax.rem(p + k, PLANES)
        lo, hi = tiles[t]
        return remote(
            feed_ref.at[q, :, :, lo:hi],
            weights.at[:, p, i, :, lo:hi],
            cross_send.at[t, k],
            cross_recv.at[t, k],
            dp=here.dp(q, i),
        )

    def cross_arrive(k, t):
        lo, hi = tiles[t]
        landed = weights.at[:, here.plane_back(k), i, :, lo:hi]
        remote(landed, landed, cross_send.at[t, k], cross_recv.at[t, k], dp=here.right).wait_recv()
        feed_rings[k][t].start()
        if t + 1 < len(tiles):
            cross(k, t + 1).start()

    def pair(k, src, dst):
        return remote(src, dst, pair_send.at[k], pair_recv.at[k], tensor=other)

    def back_pair(r):
        q = here.plane_back(r)
        return pair(r, back_low_ref if r == 0 else backs.at[q, c], backs.at[q, c])

    def back_arrive(d):
        for way in range(2):
            back_line.arrive(way, d, lambda r: back_pair(r).start())

    small_pair = pair(PLANES, small_land.at[c], small_land.at[c])
    normed_pair = pair(PLANES + 1, normed.at[c], normed.at[c])
    branch_pair = pair(PLANES + 2, branch_send, mid_sum)

    def token_pair(r):
        q = here.plane_back(r)
        return pair(PLANES + 3 + r, tokens.at[q, c], tokens.at[q, c])

    def token_arrive(d):
        for way in range(2):
            token_line.arrive(way, d, lambda r: token_pair(r).start())

    def part_pair(k):
        q = near[PLANES - 1 - k]
        return pair(2 * PLANES + 3 + k, part.at[q, other], part_land.at[q])

    def wait_pair(k, landed):
        pair(k, landed, landed).wait_recv()


    small_line.start()
    attn_line.start()
    small_rings[0].start()
    attn_rings[0].start()
    for way, d in line_order():
        small_line.arrive(way, d, lambda r: small_rings[r].start())
        attn_line.arrive(way, d, lambda r: attn_rings[r].start())
        if d == 2 and way == 1:
            for k in (1, 3, 2):
                cross(k, 0).start()
            back_line.start()
            back_pair(0).start()
    feed_rings[0][0].start()
    for r in (0, 1, 3, 2):
        small_rings[r].arrive(1)
        attn_rings[r].arrive(1)
    for r in range(PLANES):
        small_rings[r].arrive(2)
    for keep in keeps:
        keep.wait()
    small_pair.start()
    wait_pair(PLANES, small_land.at[other])
    tile = small_land.shape[-2:]
    small_wide = jnp.zeros((tile[0], LANES), F32)
    small_row[...] = jnp.zeros_like(small_row)
    for k in range(2 * PLANES * RING):
        start = k * small_n // LANES * LANES
        stop = min(start + tile[1] + LANES, small_row.shape[1])
        piece = jnp.concatenate([small_land[k % 2, k // (2 * RING), k // 2 % RING], small_wide], 1)
        piece = pltpu.roll(piece, k * small_n - start, 1)
        small_row[:, start:stop] = small_row[:, start:stop] + piece[:, : stop - start]

    x = x_ref[...]
    inv = lax.rsqrt(jnp.mean(x * x, axis=1, keepdims=True) + NORM_EPS)
    normed[c] = (x * inv * small_row[0:1, :width]).astype(BF16)
    normed_pair.start()
    back_arrive(1)
    cross_arrive(1, 0)
    middle = layer_out
    span, depth = width // PLANES, rows // 2
    near_first = (0, 1, 3, 2)

    def attention(attn_w):
        loads = []
        for r in near_first:
            attn_rings[r].arrive(2)
            q = here.plane_back(r)
            loads.append(pltpu.make_async_copy(attn_hbm.at[q], attn_w.at[q], load_sem.at[r]))
            loads[-1].start()
        wait_pair(PLANES + 1, normed.at[other])
        for load in loads:
            load.wait()

        def project(k):
            two = 2 * HD
            w = attn_w[:, :, :, k * two : (k + 1) * two].reshape(width, two)
            bias = small_row[0:1, pl.ds(pl.multiple_of(2 * width + c * cols + k * two, two), two)]
            out = dot(normed[...].reshape(2 * rows, width), w, ((1,), (0,))) + bias
            cosine, sine = cos_ref[...], sin_ref[...]
            first, second = out[:, :HD], out[:, HD:]
            first = turn(first, cosine, sine)
            if 2 * k < heads:
                second = turn(second, cosine, sine)
            qkv[:, k * two : (k + 1) * two] = jnp.concatenate([first, second], 1).astype(BF16)

        def attend(j):
            query = qkv[:, j * HD : (j + 1) * HD]
            key = qkv[:, heads * HD : (heads + 1) * HD]
            value = qkv[:, (heads + 1) * HD : (heads + 2) * HD]
            scores = dot(query, key, ((1,), (1,))) * HD ** (-0.5) + mask_ref[...]
            powers = jnp.exp(scores - jnp.max(scores, axis=1, keepdims=True))
            probs = (powers * (1.0 / jnp.sum(powers, axis=1, keepdims=True))).astype(BF16)
            out = dot(probs, value, ((1,), (0,))).astype(BF16)
            attended[:, :, j * HD : (j + 1) * HD] = out.reshape(2, rows, HD)

        def branch(t, q):
            w = attn_w[q, :, :, cols:].reshape(width // PLANES, heads * HD)
            return dot(attended[t], w, ((1,), (1,)))

        for k in range(cols // (2 * HD)):
            project(k)
            if k == 1:
                cross_arrive(3, 0)
            if k == 3:
                feed_rings[0][0].arrive(1)
        for j in range(heads):
            attend(j)
            if j == 0:
                back_arrive(2)
            if j == 1:
                cross_arrive(2, 0)
            if j == 2:
                feed_rings[1][0].arrive(1)
            if j == 3:
                feed_rings[3][0].arrive(1)
            if j == 4:
                feed_rings[0][1].start()
        for q in range(PLANES):
            branch_send[:, q * span : (q + 1) * span] = branch(other, q)
        branch_pair.start()
        feed_rings[2][0].arrive(1)
        for q in range(PLANES):
            at = slice(q * span, (q + 1) * span)
            middle[:, at] = x_ref[:, at] + branch(c, q)
        cross_arrive(1, 1)
        wait_pair(PLANES + 2, mid_sum)
        mid = middle[...] + mid_sum[...]
        middle[...] = mid
        inv = lax.rsqrt(jnp.mean(mid * mid, axis=1, keepdims=True) + NORM_EPS)
        tokens[p, c] = (mid * inv * small_row[0:1, width : 2 * width]).astype(BF16)

    pl.run_scoped(attention, pltpu.VMEM(attn_hbm.shape, BF16))

    token_line.start()
    token_pair(0).start()
    cross_arrive(3, 1)
    back_arrive(3)
    for r in range(PLANES):
        wait_pair(r, backs.at[here.plane_back(r), other])
    for r in near_first:
        feed_rings[r][0].arrive(2)
    cross_arrive(2, 1)

    mid_line = LineSum(
        here,
        lambda q: part[q, c].astype(F32) + part_land[q].astype(F32),
        lambda way, d: part_line.at[way, d - 1],
        line_send.at[4],
        line_recv.at[4],
    )

    def line_step(line, d):
        for way in range(2):
            line.step(way, d)

    def block(ref, q, j, n):
        at = pl.ds(pl.multiple_of(lax.rem(j, 2) * depth, depth), depth)
        return ref.at[q, lax.div(j, 2), at, 0:n]

    heads_cols = heads * HD
    order = (2, 1, 3, 0)
    feed_sums, qkv_sums, out_sums, small_sums, near_loads = {}, {}, {}, {}, {}
    for r in range(PLANES):
        q = here.plane_back(r)

        def sems(kind):
            return sum_send.at[kind, r], sum_recv.at[kind, r]

        feed_sums[r] = FarRingSum(
            here,
            r,
            lambda j, q=q: grads_hbm.at[:, q, j],
            weights.at[:, r, 1],
            grads_land.at[r],
            *sems(0),
            sum_load.at[0, r],
        )
        feed_sums[r].nearby, feed_sums[r].own = weights.at[:, r, 0], weights.at[:, r, 2]
        near_loads[r] = [
            pltpu.make_async_copy(grads_hbm.at[:, q, j], weights.at[:, r, k], load_sem.at[2 * r + k // 2])
            for j, k in ((feed_sums[r].next_long(), 0), (i, 2))
        ]
        for kind, sums, ref, n, land in (
            (1, qkv_sums, part, cols, qkv_land),
            (2, out_sums, backs, heads_cols, out_land),
        ):
            sums[r] = FarRingSum(
                here,
                r,
                lambda j, q=q, ref=ref, n=n: block(ref, q, j, n),
                weights.at[kind, 0, r, :, 0:n],
                land.at[r],
                *sems(kind),
                sum_load.at[kind, r],
            )
            sums[r].nearby = block(ref, q, sums[r].next_long(), n)
            sums[r].own = block(ref, q, i, n)
        small_sums[r] = RingSum(
            here,
            r,
            lambda j, q=q: small_part.at[c, q, j],
            None,
            small_part.at[c, q, i],
            small_ring_land.at[r],
            *sems(3),
        )
        small_sums[r].nearby = small_part.at[c, q, small_sums[r].next_long()]

    def feed_forward(hidden, d_gate, d_up):
        def weight(m, lo, hi):
            return weights[m, :, :, :, lo:hi].reshape(width, hi - lo)

        def feed_tile(t, q):
            lo, hi = tiles[t]
            rows_in = tokens[q].reshape(2 * rows, width)
            gate = dot(rows_in, weight(0, lo, hi), ((1,), (0,)))
            up = dot(rows_in, weight(1, lo, hi), ((1,), (0,)))
            d_hidden = dot(backs[q].reshape(2 * rows, width), weight(2, lo, hi), ((1,), (0,)))
            sig = 1.0 / (1.0 + jnp.exp(-gate))
            act = gate * sig
            hidden[q, :, lo:hi] = (act * up).astype(BF16)
            d_gate[q, :, lo:hi] = (d_hidden * up * sig * (1.0 + gate * (1.0 - sig))).astype(BF16)
            d_up[q, :, lo:hi] = (d_hidden * act).astype(BF16)

        for t in range(len(tiles)):
            if t:
                for r in near_first:
                    feed_rings[r][t].arrive(2)
            for k in range(PLANES):
                q = near[k]
                if t == 0:
                    if k:
                        token_arrive(k)
                    back = lax.rem(p + PLANES - q, PLANES)
                    wait_pair(PLANES + 3 + back, tokens.at[q, other])
                feed_tile(t, q)
                if t == 0:
                    feed_rings[near_first[k]][1].arrive(1)
                    if k == 2:
                        feed_rings[0][2].start()
                        cross_arrive(1, 2)
                    if k == 3:
                        cross_arrive(3, 2)
                if t == 1:
                    if k == 0:
                        cross_arrive(2, 2)
                    feed_rings[near_first[k]][2].arrive(1)

        def mid_chunk(k):
            q = near[PLANES - 1 - k]
            for h in range(2):
                two = slice(2 * h, 2 * h + 2)
                w_gate = weights[0, two].reshape(2 * span, -1)
                w_up = weights[1, two].reshape(2 * span, -1)
                out = dot(d_gate[q], w_gate, ((1,), (1,))) + dot(d_up[q], w_up, ((1,), (1,)))
                part[q, :, :, 2 * h * span : 2 * (h + 1) * span] = out.reshape(2, rows, 2 * span).astype(BF16)
            part_pair(k).start()

        def wait_part(k):
            wait_pair(2 * PLANES + 3 + k, part_land.at[near[PLANES - 1 - k]])

        def grad_tiles(r, early):
            q = here.plane_back(r)
            at = pl.ds(pl.multiple_of(q * span, span), span)
            copies = []
            for m in range(3):
                left = (tokens, tokens, backs)[m]
                right = (d_gate, d_up, hidden)[m]
                left = left[:, :, :, at].reshape(2 * rows * PLANES, span)
                out = dot(left, right[...].reshape(2 * rows * PLANES, -1), ((0,), (0,))).astype(BF16)
                cols_out = out.shape[1]
                if early:
                    part[m, :, :, 0:cols_out] = out.reshape(2, rows, cols_out)
                    pieces = [
                        (part.at[m, j // 2, j % 2 * depth : (j % 2 + 1) * depth, 0:cols_out], grads_hbm.at[m, q, j])
                        for j in range(RING)
                    ]
                else:
                    slot = (3 * r + m) % (2 * PLANES)
                    slot = weights.at[slot // PLANES, slot % PLANES]
                    slot[...] = out.reshape(slot.shape)
                    pieces = [(slot, grads_hbm.at[m, q])]
                for k, (src, dst) in enumerate(pieces):
                    copies.append(pltpu.make_async_copy(src, dst, stage_sem.at[m, k]))
                    copies[-1].start()
            for copy in copies:
                copy.wait()
            if r:
                feed_sums[r].start()

        def out_chunk(q):
            for h in range(2):
                w_down = weights[2, 2 * h : 2 * h + 2].reshape(2 * span, -1)
                out = dot(hidden[q], w_down, ((1,), (1,)))
                tokens[q, :, :, 2 * h * span : 2 * (h + 1) * span] = out.reshape(2, rows, 2 * span).astype(
                    BF16
                )

        grad_tiles(1, True)
        grad_tiles(3, True)
        mid_chunk(0)
        mid_chunk(1)
        wait_part(0)
        line_step(mid_line, 3)
        mid_chunk(2)
        mid_chunk(3)
        wait_part(1)
        line_step(mid_line, 2)
        for r in range(PLANES):
            for t in range(len(tiles)):
                feed_rings[r][t].finish()
        grad_tiles(2, False)
        wait_part(2)
        line_step(mid_line, 1)
        wait_part(3)
        grad_tiles(0, False)
        token_line.finish()
        for r in range(PLANES):
            token_pair(r).wait_send()
        for q in range(PLANES):
            out_chunk(q)
        mid_line.result(mid_sum)

    by_plane = pltpu.VMEM((PLANES, 2 * rows, weights.shape[-1]), BF16)
    pl.run_scoped(feed_forward, by_plane, by_plane, by_plane)

    back_line.finish()
    for r in range(PLANES):
        back_pair(r).wait_send()
        for t in range(len(tiles)):
            if r:
                cross(r, t).wait_send()
    branch_pair.wait_send()

    mid_line.finish()
    for q in range(PLANES):
        part_pair(q).wait_send()
    pl.semaphore_signal(ready_sem.at[0], inc=1, device_id={"tensor": other}, device_id_type=MESH)
    for k, exists, dp in ((1, p + 1 < PLANES, here.above), (2, p > 0, here.below)):

        @pl.when(exists)
        def _():
            pl.semaphore_signal(ready_sem.at[k], inc=1, device_id={"dp": dp}, device_id_type=MESH)

    pl.semaphore_wait(ready_sem.at[0], 1)
    for k, exists in ((2, p + 1 < PLANES), (1, p > 0)):

        @pl.when(exists)
        def _():
            pl.semaphore_wait(ready_sem.at[k], 1)

    def feed_pair(q):
        return pair(3 * PLANES + 3 + q, tokens.at[q, other], part_land.at[q])

    feed_line = LineSum(
        here,
        lambda q: tokens[q, c].astype(F32) + part_land[q].astype(F32),
        lambda way, d: part_line.at[way, d - 1],
        line_send.at[5],
        line_recv.at[5],
    )
    branch_all_pair = pair(4 * PLANES + 3, branch_all.at[c], branch_all.at[c])
    d_normed_pair = pair(4 * PLANES + 4, branch_send, input_grad)
    small_grad_pair = pair(4 * PLANES + 5, small_part.at[other], small_pair_land)

    def feed_cross(r):
        q = here.plane_back(r)
        return remote(
            weights.at[:, r, 2], feed_new.at[p], cross_send.at[3, r], cross_recv.at[3, r], dp=here.dp(q, i)
        )

    def feed_step(r):
        near_loads[r][0].wait()
        feed_sums[r].step()

    feed_own = pltpu.make_async_copy(weights.at[:, 0, 2], feed_new.at[p], keep_sem.at[0])

    def feed_result(r):
        near_loads[r][1].wait()
        total = feed_sums[r].result(weights.at[:, r, 0], weights.at[:, r, 3])
        weights[:, r, 2] = total.astype(BF16)
        if r:
            feed_cross(r).start()
        else:
            feed_own.start()

    def backward(w_half, d_keys, d_values, qkv_plane, out_plane, back_rows, d_attended, d_projected):
        load_out = pltpu.make_async_copy(
            attn_hbm.at[:, :, :, cols:], w_half.at[:, :, :, :heads_cols], keep_sem.at[1]
        )
        load_qkv = pltpu.make_async_copy(attn_hbm.at[:, :, :, :cols], w_half, keep_sem.at[2])
        load_back = pltpu.make_async_copy(back_ref, back_rows, keep_sem.at[3])
        load_back.start()
        load_out.start()
        for r in (1, 3, 2):
            for load in near_loads[r]:
                load.start()

        mid = middle[...]
        inv = lax.rsqrt(jnp.mean(mid * mid, axis=1, keepdims=True) + NORM_EPS)
        unit = mid * inv
        grad = mid_sum[...]
        gain_row[...] = jnp.zeros_like(gain_row)
        gain_row[:, width : 2 * width] = fold(grad * unit)
        grad = grad * small_row[0:1, width : 2 * width]
        load_back.wait()
        grad = back_rows[...] + inv * (grad - unit * jnp.mean(grad * unit, axis=1, keepdims=True))
        mid_sum[...] = grad
        branch_all[c] = grad.astype(BF16)
        branch_all_pair.start()
        for q in range(PLANES):
            feed_pair(q).start()
        feed_step(1)
        load_out.wait()
        wait_pair(4 * PLANES + 3, branch_all.at[other])

        for n in range(heads_cols // 256):
            at = slice(n * 256, (n + 1) * 256)
            w = w_half[:, :, :, at].reshape(width, 256)
            out = dot(branch_all[...].reshape(2 * rows, width), w, ((1,), (0,)))
            d_attended[:, at] = out.astype(BF16)
        load_qkv.start()
        for q in range(PLANES):
            feed_pair(q).wait_recv()
        line_step(feed_line, 3)
        feed_step(3)
        for r in order:
            q = here.plane_back(r)
            at = pl.ds(pl.multiple_of(q * span, span), span)
            out = dot(
                branch_all[:, :, at].reshape(2 * rows, span),
                attended[...].reshape(2 * rows, -1),
                ((0,), (0,)),
            )
            backs[q, :, :, 0:heads_cols] = out.reshape(2, rows, heads_cols).astype(BF16)
            out_sums[r].start()
        scale = HD ** (-0.5)

        def attend_back(j):
            at = slice(j * HD, (j + 1) * HD)
            query, d_out = qkv[:, at], d_attended[:, at]
            key = qkv[:, heads * HD : (heads + 1) * HD]
            value = qkv[:, (heads + 1) * HD : (heads + 2) * HD]
            scores = dot(query, key, ((1,), (1,))) * scale + mask_ref[...]
            powers = jnp.exp(scores - jnp.max(scores, axis=1, keepdims=True))
            probs = powers * (1.0 / jnp.sum(powers, axis=1, keepdims=True))
            d_probs = dot(d_out, value, ((1,), (1,)))
            d_value = dot(probs.astype(BF16), d_out, ((0,), (0,)))
            d_scores = probs * (d_probs - jnp.sum(probs * d_probs, axis=1, keepdims=True))
            d_scores = d_scores.astype(BF16)
            d_query = dot(d_scores, key, ((1,), (0,))) * scale
            d_key = dot(d_scores, query, ((0,), (0,))) * scale
            d_projected[:, at] = turn_back(d_query, cos_ref[...], sin_ref[...]).astype(BF16)
            if j:
                d_value = d_values[...] + d_value
                d_key = d_keys[...] + d_key
            d_values[...] = d_value
            d_keys[...] = d_key

        for j in range(heads):
            attend_back(j)
            if j == 1:
                feed_step(2)
            if j == 3:
                line_step(feed_line, 2)
            if j == 4:
                feed_result(1)
            if j == 5:
                feed_result(3)
        d_key = turn_back(d_keys[...], cos_ref[...], sin_ref[...])
        d_projected[:, heads_cols:] = jnp.concatenate([d_key, d_values[...]], 1).astype(BF16)
        gain_row[:, pl.ds(pl.multiple_of(2 * width + c * cols, cols), cols)] = fold(
            d_projected[...].astype(F32)
        )
        for r in order:
            q = here.plane_back(r)
            at = pl.ds(pl.multiple_of(q * span, span), span)
            out = dot(normed[:, :, at].reshape(2 * rows, span), d_projected[...], ((0,), (0,)))
            part[q, :, :, 0:cols] = out.reshape(2, rows, cols).astype(BF16)
            qkv_sums[r].start()
        for r in order:
            out_sums[r].step()
        load_qkv.wait()

        def d_normed(t, q):
            w = w_half[q].reshape(span, cols)
            at = pl.ds(pl.multiple_of(t * rows, rows), rows)
            return dot(d_projected[at, :], w, ((1,), (1,)))

        for q in range(PLANES):
            branch_send[:, q * span : (q + 1) * span] = d_normed(other, q)
        d_normed_pair.start()
        mine = jnp.concatenate([d_normed(c, q) for q in range(PLANES)], 1)
        feed_result(2)
        d_normed_pair.wait_recv()
        grad = mine + input_grad[...]
        x = x_ref[...]
        inv = lax.rsqrt(jnp.mean(x * x, axis=1, keepdims=True) + NORM_EPS)
        unit = x * inv
        gain_row[:, :width] = fold(grad * unit)
        grad = grad * small_row[0:1, :width]
        input_grad[...] = mid_sum[...] + inv * (grad - unit * jnp.mean(grad * unit, axis=1, keepdims=True))

        tile = small_part.shape[-2:]
        inside = lax.broadcasted_iota(jnp.int32, tile, 1) < small_n
        for k in range(2 * PLANES * RING):
            start = k * small_n // LANES * LANES
            piece = gain_row[:, start : start + tile[1] + LANES]
            piece = pltpu.roll(piece, (start - k * small_n) % piece.shape[1], 1)[:, : tile[1]]
            small_part[k % 2, k // (2 * RING), k // 2 % RING] = jnp.where(inside, piece, 0.0)
        small_grad_pair.start()
        for r in order:
            qkv_sums[r].step()
        feed_sums[0].start()
        line_step(feed_line, 1)
        small_grad_pair.wait_recv()
        small_part[c] = small_part[c] + small_pair_land[...]
        for r in order:
            small_sums[r].start()
        for r in order:
            small_sums[r].step()
        for r in order:
            q = here.plane_back(r)
            small_plane[q] = small_sums[r].result()
            for sums, plane, second in (
                (qkv_sums, qkv_plane, weights.at[0, 0, r, :, 0:cols]),
                (out_sums, out_plane, d_attended.at[r * depth : (r + 1) * depth]),
            ):
                sums[r].copy(1).wait_send()
                plane[q] = sums[r].result(sums[r].passing, second)
        lines = []
        for k, plane, land in ((6, qkv_plane, qkv_line_land), (7, out_plane, out_line_land)):
            lines.append(
                LineSum(
                    here,
                    lambda q, plane=plane: plane[q],
                    lambda way, d, land=land: land.at[way, d - 1],
                    line_send.at[k],
                    line_recv.at[k],
                )
            )
        small_line = SmallLine(here, small_plane, small_line_land, small_send, small_recv)
        small_line.start()
        for load in near_loads[0]:
            load.start()
        for d in range(PLANES - 1, 0, -1):
            for line in lines:
                line_step(line, d)
            if d == 3:
                feed_step(0)
                feed_line.result(back_rows)
                layer_out[...] = (middle[...] + back_rows[...]) * live_ref[:, 0:1]
        feed_line.finish()
        small_line.result(small_sum)
        for line, out in zip(lines, (qkv_sum, out_sum)):
            line.result(out)
            line.finish()
        feed_result(0)
        small_line.finish()

    pl.run_scoped(
        backward,
        pltpu.VMEM(attn_hbm.shape[:3] + (cols,), BF16),
        pltpu.VMEM((2 * rows, HD), F32),
        pltpu.VMEM((2 * rows, HD), F32),
        pltpu.VMEM((PLANES,) + qkv_sum.shape, F32),
        pltpu.VMEM((PLANES,) + out_sum.shape, F32),
        pltpu.VMEM((rows, width), F32),
        pltpu.VMEM((2 * rows, heads_cols), BF16),
        pltpu.VMEM((2 * rows, cols), BF16),
    )

    for r in (1, 3, 2):
        landed = feed_new.at[lax.rem(p + r, PLANES)]
        remote(landed, landed, cross_send.at[3, r], cross_recv.at[3, r], dp=here.right).wait_recv()
    feed_own.wait()
    for flow in [small_line, attn_line] + small_rings + attn_rings:
        flow.finish()
    for r in range(PLANES):
        feed_pair(r).wait_send()
        feed_sums[r].finish()
        small_sums[r].finish()
        qkv_sums[r].finish(False)
        out_sums[r].finish(False)
        if r:
            feed_cross(r).wait_send()
    for copy in (small_pair, normed_pair, branch_all_pair, d_normed_pair, small_grad_pair):
        copy.wait_send()


class SmallLine:
    def __init__(self, here, addends, landing, send, recv):
        self.here, self.addends, self.landing, self.send, self.recv = here, addends, landing, send, recv

    def copy(self, k):
        here = self.here
        q = lax.rem(here.plane + k, PLANES)
        return remote(
            self.addends.at[q], self.landing.at[k], self.send.at[k], self.recv.at[k], dp=here.dp(q, here.index)
        )

    def start(self):
        for k in range(1, PLANES):
            self.copy(k).start()

    def result(self, out):
        total = self.addends[self.here.plane]
        for k in range(1, PLANES):
            self.copy(k).wait_recv()
            total = total + self.landing[k]
        out[...] = total

    def finish(self):
        for k in range(1, PLANES):
            self.copy(k).wait_send()


ANY = pl.BlockSpec(memory_space=pl.ANY)
VMEM = pl.BlockSpec(memory_space=pltpu.VMEM)
DMA = pltpu.SemaphoreType.DMA


def kernel_params(number, mib=None):
    return pltpu.CompilerParams(
        collective_id=number, has_side_effects=True, vmem_limit_bytes=None if mib is None else mib * MIB
    )


def layer(members, small, attn, feed, back_low, back, rows_in, tables, live):
    depth, cols = attn.shape
    part = feed.shape[3]
    rows, width = rows_in.shape
    out_cols = width // 2
    head_cols = cols - out_cols
    by_rows = (PLANES, 2, rows, width)
    tile = small.shape
    small_all = 2 * width + 2 * head_cols

    def hbm(*shape):
        return jax.ShapeDtypeStruct(shape, BF16)

    return pl.pallas_call(
        functools.partial(layer_kernel, members),
        out_shape=(
            jax.ShapeDtypeStruct((rows, width), F32),
            jax.ShapeDtypeStruct((rows, width), F32),
            jax.ShapeDtypeStruct(tile, F32),
            jax.ShapeDtypeStruct((depth, head_cols), F32),
            jax.ShapeDtypeStruct((depth, out_cols), F32),
            hbm(PLANES, 3, depth, part),
            hbm(PLANES, RING, depth, cols),
            hbm(3, PLANES, RING, depth, part),
            hbm(PLANES, 3, 3, depth, part),
            hbm(PLANES, 3, depth, head_cols),
            hbm(PLANES, 3, depth, out_cols),
        ),
        in_specs=[ANY] * 5 + [VMEM] * 5,
        out_specs=(VMEM,) * 5 + (ANY,) * 6,
        scratch_shapes=[
            pltpu.VMEM((8, small_all), F32),
            pltpu.VMEM((2, rows, width), BF16),
            pltpu.VMEM((2 * rows, head_cols), BF16),
            pltpu.VMEM((2, rows, out_cols), BF16),
            pltpu.VMEM((rows, width), F32),
            pltpu.VMEM((2, PLANES, RING) + tile, F32),
            pltpu.VMEM((3, PLANES, RING, depth, part), BF16),
            pltpu.VMEM(by_rows, BF16),
            pltpu.VMEM(by_rows, BF16),
            pltpu.VMEM((rows, width), F32),
            pltpu.VMEM(by_rows, BF16),
            pltpu.VMEM((PLANES, rows, width), BF16),
            pltpu.VMEM((2, PLANES - 1, rows, width), BF16),
            pltpu.VMEM((2, rows, width), BF16),
            pltpu.VMEM((2, PLANES - 1, depth, head_cols), BF16),
            pltpu.VMEM((2, PLANES - 1, depth, out_cols), BF16),
            pltpu.VMEM((8, small_all + 2 * LANES), F32),
            pltpu.VMEM((2, PLANES, RING) + tile, F32),
            pltpu.VMEM((PLANES, RING) + tile, F32),
            pltpu.VMEM((PLANES, 3) + tile, F32),
            pltpu.VMEM((PLANES,) + tile, F32),
            pltpu.VMEM((PLANES,) + tile, F32),
            pltpu.SemaphoreType.REGULAR((3,)),
            DMA((8, 2, PLANES)),
            DMA((8, 2, PLANES)),
            DMA((2, PLANES, 2, RING)),
            DMA((2, PLANES, 2, RING)),
            DMA((3, PLANES, 2, RING)),
            DMA((3, PLANES, 2, RING)),
            DMA((4, PLANES)),
            DMA((4, PLANES)),
            DMA((4 * PLANES + 6,)),
            DMA((4 * PLANES + 6,)),
            DMA((4, PLANES, 3)),
            DMA((4, PLANES, 3)),
            DMA((3, PLANES, 3)),
            DMA((PLANES,)),
            DMA((PLANES,)),
            DMA((4,)),
            DMA((2 * PLANES,)),
            DMA((3, RING)),
        ],
        compiler_params=kernel_params(0, 63),
        name="layer",
    )(small, attn, feed, back_low, back, rows_in, *tables, live)


def take(x, index):
    return lax.dynamic_index_in_dim(x, index, 0, keepdims=False)


def member_groups(members):
    return [list(range(g * members, (g + 1) * members)) for g in range(PLANES * RING)]


def member_gather(x, members, axis):
    return lax.all_gather(
        x, "dp", axis=axis, tiled=True, axis_index_groups=member_groups(members)
    )


def member_sums(members, small, qkv, out, feed):
    groups = member_groups(members)
    qkv = lax.psum_scatter(qkv, "dp", scatter_dimension=0, tiled=True, axis_index_groups=groups)
    out = lax.psum_scatter(out, "dp", scatter_dimension=0, tiled=True, axis_index_groups=groups)
    feed = lax.psum_scatter(feed, "dp", scatter_dimension=2, tiled=True, axis_index_groups=groups)
    small = lax.psum(small, "dp", axis_index_groups=groups)
    small = lax.all_gather(small, "tensor", axis=0, tiled=True)
    share = small.shape[0] // (2 * members)
    at = (lax.axis_index("dp") % members * 2 + lax.axis_index("tensor")) * share
    return lax.dynamic_slice_in_dim(small, at, share, 0), qkv, out, feed


def row_major(x):
    return with_layout_constraint(x, Layout(major_to_minor=(0, 1, 2)))


def make_shards(members):
    def shards(
        layer_input,
        output_grad,
        seq_lengths,
        gains_biases,
        gains_moment,
        gains_second,
        qkv_weight,
        qkv_moment,
        qkv_second,
        out_weight,
        out_moment,
        out_second,
        gate_up_weight,
        gate_up_moment,
        gate_up_second,
        down_weight,
        down_moment,
        down_second,
    ):
        core = lax.axis_index("tensor")
        rows_here, width = layer_input.shape
        buffer_rows = 2 * rows_here
        depth = qkv_weight.shape[0]
        group_cols = qkv_weight.shape[2]
        head_dim = HD
        hidden_here = down_weight.shape[1]
        part = -(-hidden_here // (PLANES * LANES)) * LANES
        spare = PLANES * part - hidden_here

        segment, position, live_rows = layout(seq_lengths[0], buffer_rows)
        live_here = lax.dynamic_slice_in_dim(live_rows, core * rows_here, rows_here, 0)[:, None]
        cosine_table, sine_table = rotary(position, head_dim)
        row_order = jnp.arange(buffer_rows, dtype=jnp.int32)
        allowed = (segment[:, None] == segment[None, :]) & (row_order[None, :] <= row_order[:, None])

        back_rows = output_grad * live_here

        attn = jnp.concatenate([qkv_weight[:, 0], out_weight], 1).astype(BF16)
        feed = jnp.stack([gate_up_weight[:, 0], gate_up_weight[:, 1], down_weight]).astype(BF16)
        feed = jnp.pad(feed, ((0, 0), (0, 0), (0, spare)))
        feed = jnp.moveaxis(feed.reshape(3, depth, PLANES, part), 2, 0)
        small_n = gains_biases.shape[0] * members
        small = gains_biases
        if members > 1:
            attn = member_gather(attn, members, 0)
            feed = member_gather(feed, members, 2)
            small = lax.all_gather(small, ("dp", "tensor"), axis=0, tiled=True)
            group = lax.axis_index("dp") // members
            small = lax.dynamic_slice_in_dim(small, (group * 2 + core) * small_n, small_n, 0)
        depth = depth * members
        small = jnp.broadcast_to(jnp.pad(small, (0, 2 * LANES - small_n)), (8, 2 * LANES))
        half_sign = jnp.where(jnp.arange(head_dim) < head_dim // 2, -1.0, 1.0)
        tables = (cosine_table, sine_table * half_sign, jnp.where(allowed, 0.0, MASK_VALUE))
        live = jnp.broadcast_to(live_here, (rows_here, LANES))
        layer_output, input_grad, small_shard, qkv_shard, out_shard, feed_new = layer(
            members, small, attn, feed, back_rows.astype(BF16), back_rows, layer_input, tables, live
        )[:6]
        small_shard = jnp.sum(small_shard, axis=0)[:small_n]
        if members > 1:
            small_shard, qkv_shard, out_shard, feed_new = member_sums(
                members, small_shard, qkv_shard, out_shard, feed_new
            )
            depth = depth // members
        feed_new = jnp.moveaxis(feed_new.astype(F32), 0, 2).reshape(3, depth, PLANES * part)[:, :, :hidden_here]
        gate_up_shard = jnp.stack([feed_new[0], feed_new[1]], 1)
        qkv_shard = row_major(qkv_shard[:, None])
        down_shard = feed_new[2]

        small_out = adam_update(
            gains_biases, gains_moment, gains_second, small_shard, RATE_SMALL, 0.0
        )
        qkv_out = adam_update(
            qkv_weight, qkv_moment, qkv_second, qkv_shard, RATE_PROJECT, WEIGHT_DECAY
        )
        out_out = adam_update(
            out_weight, out_moment, out_second, out_shard, RATE_OUTPUT, WEIGHT_DECAY
        )
        gate_up_out = adam_update(
            gate_up_weight, gate_up_moment, gate_up_second, gate_up_shard, RATE_FEED, WEIGHT_DECAY
        )
        down_out = adam_update(
            down_weight, down_moment, down_second, down_shard, RATE_DOWN, WEIGHT_DECAY
        )
        return (layer_output, input_grad, *small_out, *qkv_out, *out_out, *gate_up_out, *down_out)

    return shards


def solution(mesh):
    rows = P(("dp", "tensor"), None)
    small = P(("dp", "tensor"))
    qkv = P("dp", "tensor", None)
    flat = P("dp", "tensor")
    gate_up = P("dp", None, "tensor")
    weights = (small,) * 3 + (qkv,) * 3 + (flat,) * 3 + (gate_up,) * 3 + (flat,) * 3
    return jax.shard_map(
        make_shards(mesh.shape["dp"] // (PLANES * RING)),
        mesh=mesh,
        in_specs=(rows, rows, P("dp", None)) + weights,
        out_specs=(rows, rows) + weights,
        check_vma=False,
    )
```
